32 devices in a mesh: ctx: 16 (over z, y, core), head: 2 (over x).
Axes of the slice: x: 2, y: 2, z: 4, core: 2. Of those that a mesh axis runs over, the one named last changes fastest.
Arguments:
- tokens: bfloat16 [8192, 3840], P('ctx', 'head'), may hold values from -18 to 18
- w_query: bfloat16 [3840, 4096], P('ctx', 'head'), may hold values from -0.09375 to 0.09375
- key_matrix: bfloat16 [3840, 2048], P('ctx', 'head'), may hold values from -0.09375 to 0.09375
- value_matrix: bfloat16 [3840, 2048], P('ctx', 'head'), may hold values from -0.09375 to 0.09375
- d_attended: bfloat16 [8192, 4096], P('ctx', 'head'), may hold values from -6 to 6
- doc_lengths: int32 [8], replicated, may hold values from 1 to 2048, 8192 in all
Outputs:
- attended: bfloat16 [8192, 4096], P('ctx', 'head')
- key_grad: bfloat16 [8192, 2048], P('ctx', 'head')
The draws below stay inside these ranges and needn't reach their ends.
Inputs may be any that keep to these rules, and one draw needn't show every extreme that they name: `doc_lengths`: the documents lie end to end from position 0 and fill all 8192 positions.
All inputs are finite; a program needn't handle non-finite values.
Results may differ from the reference program's by a relative error of at most 0.012.
The reference program's roundings to bfloat16 on the way (of `query`, `probs_low` and `dscore`) count: a program that leaves them out, or rounds other values in their place, can miss the bound.
Values may be sent and summed in bfloat16 or wider, within the bound.
A program may use at most 128 MiB of HBM per device.

```python
import math
import jax
import jax.numpy as jnp
import numpy as np
from jax import lax

MODEL_WIDTH = 3840
HQ = 16
KEY_VALUE_HEADS = 8
HEAD_SIZE = 256
WINDOW = 1024
TOK_DEV = 512
CONTEXT_TOKENS = 8192
DOCS = 8


def draw_tokens(key, part):
    values = jax.random.truncated_normal(key, -6.0, 6.0, (CONTEXT_TOKENS, MODEL_WIDTH), jnp.float32)
    return values.astype(jnp.bfloat16)


def block_scale(rng, shape, pieces, smallest, high):
    loudness = 1.0
    for position, shards_of in pieces:
        heights = jax.random.uniform(jax.random.fold_in(jax.random.fold_in(rng, 6), position), (shards_of,), jnp.float32, smallest / len(pieces), high / len(pieces))
        loudness = loudness * jnp.repeat(jnp.exp(heights), shape[position] // shards_of).reshape((-1,) + (1,) * (len(shape) - 1 - position))
    return loudness


def profile(count, total, limit, lean):
    weights = [(1 << 20) // math.isqrt(standing ** lean) + 1 for standing in range(2, count + 1)]
    rest, counts = total - limit - (count - 1), [1] * (count - 1)
    while rest > 0:
        candidates = [i for i in range(count - 1) if counts[i] < limit]
        mass, remaining = sum([weights[i] for i in candidates]), rest
        for i in candidates:
            addition = min(limit - counts[i], max(1, remaining * weights[i] // mass), rest)
            counts[i] = counts[i] + addition
            rest = rest - addition
    return np.array([limit] + counts)


def uneven_parts(own_key, count, total, limit, skew):
    if count == 2:
        one = jax.random.randint(own_key, (), max(1, total - limit), min(limit, total - 1) + 1)
        return jnp.stack([one, total - one])
    sizes = jnp.asarray(profile(count, total, limit, skew), jnp.int32)
    twos = (count - 1) // 2
    giver, taker = sizes[1:1 + 2 * twos:2], sizes[2:2 + 2 * twos:2]
    margin = jnp.minimum(giver - 1, limit - taker)
    passed = jax.random.randint(jax.random.fold_in(own_key, 1), (twos,), 0, 1 << 20) % (margin + 1)
    sizes = sizes.at[1:1 + 2 * twos:2].set(giver - passed).at[2:2 + 2 * twos:2].set(taker + passed)
    return sizes[jax.random.permutation(jax.random.fold_in(own_key, 2), count)]


def noise(key, shape, deviation, most, pieces=(), held_as=jnp.bfloat16):
    result = deviation * jax.random.normal(key, shape, jnp.float32)
    if pieces:
        result = result * block_scale(key, shape, pieces, -0.22, 0.18)
    return jnp.clip(result, -most, most).astype(held_as)


def setup_inputs(seed: int = 0) -> dict:
    splits = jax.random.split(jax.random.key(seed), 7)
    return {
        "tokens": draw_tokens(jax.random.fold_in(splits[6], 71), 0),
        "w_query": noise(splits[1], (MODEL_WIDTH, HQ * HEAD_SIZE), MODEL_WIDTH ** -0.5, 0.09375, ((0, 16), (1, 2))),
        "key_matrix": noise(splits[2], (MODEL_WIDTH, KEY_VALUE_HEADS * HEAD_SIZE), MODEL_WIDTH ** -0.5, 0.09375, ((0, 16), (1, 2))),
        "value_matrix": noise(splits[3], (MODEL_WIDTH, KEY_VALUE_HEADS * HEAD_SIZE), MODEL_WIDTH ** -0.5, 0.09375, ((0, 16), (1, 2))),
        "d_attended": noise(splits[4], (CONTEXT_TOKENS, HQ * HEAD_SIZE), 1.0, 6.0, ((0, 16), (1, 2))),
        "doc_lengths": uneven_parts(splits[5], DOCS, CONTEXT_TOKENS, 2 * WINDOW, 2).astype(jnp.int32),
    }


def doc_begin(positions, doc_start):
    inside = doc_start[None, :] <= positions[:, None]
    return jnp.max(jnp.where(inside, doc_start[None, :], 0), axis=1)


def attend_block(query_blk, key_block, value_block, grad_blk, leading_row, doc_start):
    rows = query_blk.shape[0]
    window_length = key_block.shape[0]
    kv_heads = key_block.shape[1]
    group = query_blk.shape[1] // kv_heads
    width = query_blk.shape[2]
    query_pos = leading_row + jnp.arange(rows, dtype=jnp.int32)
    key_pos = leading_row - (window_length - rows) + jnp.arange(window_length, dtype=jnp.int32)
    begins = doc_begin(query_pos, doc_start)
    allowed = (key_pos[None, :] >= begins[:, None]) & (key_pos[None, :] <= query_pos[:, None]) & (key_pos[None, :] > query_pos[:, None] - WINDOW)
    query_four = query_blk.reshape(rows, kv_heads, group, width).astype(jnp.float32)
    grad_four = grad_blk.reshape(rows, kv_heads, group, width).astype(jnp.float32)
    key_three = key_block.astype(jnp.float32)
    value_three = value_block.astype(jnp.float32)
    scores = jnp.einsum("tgeh,sgh->gets", query_four, key_three)
    scores = jnp.where(allowed[None, None], scores, -1e30)
    peak = jnp.max(scores, axis=-1, keepdims=True)
    expo = jnp.exp(scores - peak)
    probs = expo / jnp.sum(expo, axis=-1, keepdims=True)
    probs_low = probs.astype(jnp.bfloat16)
    attended = jnp.einsum("gets,sgh->tgeh", probs_low.astype(jnp.float32), value_three)
    attended = attended.astype(jnp.bfloat16).reshape(rows, kv_heads * group * width)
    dprob = jnp.einsum("tgeh,sgh->gets", grad_four, value_three)
    delta = jnp.sum(probs * dprob, axis=-1, keepdims=True)
    dscore = (probs * (dprob - delta)).astype(jnp.bfloat16)
    key_part = jnp.einsum("gets,tgeh->sgh", dscore.astype(jnp.float32), query_four)
    return attended, key_part.reshape(window_length, kv_heads * width)


def reference(tokens, w_query, key_matrix, value_matrix, d_attended, doc_lengths):
    doc_start = (jnp.cumsum(doc_lengths) - doc_lengths).astype(jnp.int32)
    window_extent = (WINDOW // TOK_DEV) * TOK_DEV
    window_length = window_extent + TOK_DEV
    query = (jnp.dot(tokens, w_query, preferred_element_type=jnp.float32) * 0.0625).astype(jnp.bfloat16)
    keys = jnp.dot(tokens, key_matrix, preferred_element_type=jnp.float32).astype(jnp.bfloat16)
    values = jnp.dot(tokens, value_matrix, preferred_element_type=jnp.float32).astype(jnp.bfloat16)
    padded_keys = jnp.concatenate([jnp.zeros((window_extent, keys.shape[1]), jnp.bfloat16), keys], axis=0)
    padded_values = jnp.concatenate([jnp.zeros((window_extent, values.shape[1]), jnp.bfloat16), values], axis=0)

    def step(key_acc, block):
        leading_row = (block * TOK_DEV).astype(jnp.int32)
        query_blk = lax.dynamic_slice_in_dim(query, leading_row, TOK_DEV, 0).reshape(TOK_DEV, HQ, HEAD_SIZE)
        grad_blk = lax.dynamic_slice_in_dim(d_attended, leading_row, TOK_DEV, 0).reshape(TOK_DEV, HQ, HEAD_SIZE)
        key_block = lax.dynamic_slice_in_dim(padded_keys, leading_row, window_length, 0).reshape(window_length, KEY_VALUE_HEADS, HEAD_SIZE)
        value_block = lax.dynamic_slice_in_dim(padded_values, leading_row, window_length, 0).reshape(window_length, KEY_VALUE_HEADS, HEAD_SIZE)
        attended, key_part = attend_block(query_blk, key_block, value_block, grad_blk, leading_row, doc_start)
        current = lax.dynamic_slice_in_dim(key_acc, leading_row, window_length, 0)
        key_acc = lax.dynamic_update_slice_in_dim(key_acc, current + key_part, leading_row, 0)
        return key_acc, attended

    start_running = jnp.zeros((window_extent + CONTEXT_TOKENS, KEY_VALUE_HEADS * HEAD_SIZE), jnp.float32)
    key_acc, blocks_out = lax.scan(step, start_running, jnp.arange(CONTEXT_TOKENS // TOK_DEV, dtype=jnp.int32))
    attended = blocks_out.reshape(CONTEXT_TOKENS, HQ * HEAD_SIZE)
    key_grad = key_acc[window_extent:].astype(jnp.bfloat16)
    return attended, key_grad
```

```python
import functools

import jax
import jax.numpy as jnp
from jax import lax
from jax.experimental import pallas as pl
from jax.experimental.pallas import tpu as pltpu
from jax.sharding import PartitionSpec as P

HEAD_SIZE = 256
WINDOW = 1024
TILE = 128


def shifted(block, axis, distance):
    devices = range(lax.axis_size(axis))
    route = [(i - distance, i) for i in devices if i - distance in devices]
    return lax.ppermute(block, axis, route)


def attend_kernel(count, group, *refs):
    lead_ref, lengths_ref, query_ref, grad_ref = refs[:4]
    key_refs = refs[4 : 4 + count]
    value_refs = refs[4 + count : 4 + 2 * count]
    out_ref = refs[4 + 2 * count]
    sum_refs = refs[5 + 2 * count : 5 + 3 * count]
    keys, values, sums = refs[5 + 3 * count :]
    rows = query_ref.shape[0]
    docs = lengths_ref.shape[0]
    for n in range(count):
        keys[n * rows : (n + 1) * rows] = key_refs[n][...]
        values[n * rows : (n + 1) * rows] = value_refs[n][...]
    sums[...] = jnp.zeros_like(sums)
    lead = lead_ref[0]
    span = WINDOW + TILE

    def one_tile(t, carry):
        first = pl.multiple_of(t * TILE, TILE)
        window = pl.ds(first, span)
        row_pos = lead + first + lax.broadcasted_iota(jnp.int32, (TILE, 1), 0)
        key_pos = lead + first - WINDOW + lax.broadcasted_iota(jnp.int32, (1, span), 1)
        begin = jnp.zeros_like(row_pos)
        start = jnp.int32(0)
        for d in range(docs):
            begin = jnp.where(row_pos >= start, start, begin)
            start = start + lengths_ref[d]
        least = jnp.maximum(begin, row_pos - (WINDOW - 1))
        allowed = (key_pos >= least) & (key_pos <= row_pos)
        key = keys[window, :]
        value = values[window, :]
        total = sums[window, :]
        for e in range(group):
            columns = slice(e * HEAD_SIZE, (e + 1) * HEAD_SIZE)
            query = query_ref[pl.ds(first, TILE), columns]
            grad = grad_ref[pl.ds(first, TILE), columns]
            scores = lax.dot_general(
                query, key, (((1,), (1,)), ((), ())), preferred_element_type=jnp.float32
            )
            dprob = lax.dot_general(
                grad, value, (((1,), (1,)), ((), ())), preferred_element_type=jnp.float32
            )
            scores = jnp.where(allowed, scores, -1e30)
            expo = jnp.exp(scores - jnp.max(scores, axis=1, keepdims=True))
            probs = expo * (1.0 / jnp.sum(expo, axis=1, keepdims=True))
            out = jnp.dot(probs.astype(jnp.bfloat16), value, preferred_element_type=jnp.float32)
            out_ref[pl.ds(first, TILE), columns] = out.astype(jnp.bfloat16)
            delta = jnp.sum(probs * dprob, axis=1, keepdims=True)
            dscore = (probs * (dprob - delta)).astype(jnp.bfloat16)
            total = total + lax.dot_general(
                dscore, query, (((0,), (0,)), ((), ())), preferred_element_type=jnp.float32
            )
        sums[window, :] = total
        return carry

    lax.fori_loop(0, rows // TILE, one_tile, 0)
    for n in range(count):
        sum_refs[n][...] = sums[n * rows : (n + 1) * rows].astype(sum_refs[n].dtype)


def attend(query, grad_rows, joined, lead, lengths, first_head, heads):
    rows = query.shape[0]
    count = len(joined)
    kv_heads = joined[0].shape[1] // (2 * HEAD_SIZE)
    group = query.shape[1] // (kv_heads * HEAD_SIZE)
    wide = pl.BlockSpec((rows, group * HEAD_SIZE), lambda g: (0, first_head + g))
    key_spec = pl.BlockSpec((rows, HEAD_SIZE), lambda g: (0, first_head + g))
    value_spec = pl.BlockSpec((rows, HEAD_SIZE), lambda g: (0, kv_heads + first_head + g))
    sum_spec = pl.BlockSpec((rows, HEAD_SIZE), lambda g: (0, g))
    scalars = pl.BlockSpec(memory_space=pltpu.SMEM)
    kinds = [jnp.bfloat16] * (count - 1) + [jnp.float32]
    outs = pl.pallas_call(
        functools.partial(attend_kernel, count, group),
        grid=(heads,),
        in_specs=[scalars, scalars, wide, wide] + [key_spec] * count + [value_spec] * count,
        out_specs=[pl.BlockSpec((rows, group * HEAD_SIZE), lambda g: (0, g))] + [sum_spec] * count,
        out_shape=[jax.ShapeDtypeStruct((rows, heads * group * HEAD_SIZE), jnp.bfloat16)]
        + [jax.ShapeDtypeStruct((rows, heads * HEAD_SIZE), kind) for kind in kinds],
        scratch_shapes=[
            pltpu.VMEM((count * rows, HEAD_SIZE), jnp.bfloat16),
            pltpu.VMEM((count * rows, HEAD_SIZE), jnp.bfloat16),
            pltpu.VMEM((count * rows, HEAD_SIZE), jnp.float32),
        ],
        compiler_params=pltpu.CompilerParams(vmem_limit_bytes=40 * 2**20),
        cost_estimate=pl.CostEstimate(
            flops=10 * heads * group * rows * (WINDOW + TILE) * HEAD_SIZE,
            bytes_accessed=heads * rows * HEAD_SIZE * 2 * (3 * group + 5 * count),
            transcendentals=heads * group * rows * (WINDOW + TILE),
        ),
    )(lead, lengths, query, grad_rows, *joined, *joined)
    return outs[0], outs[1:]


def local(tokens, w_query, key_matrix, value_matrix, d_attended, doc_lengths):
    features = lax.all_gather(tokens, "head", axis=1, tiled=True)
    rows_here = features.shape[0]
    kv_heads = key_matrix.shape[1] // HEAD_SIZE

    def project(piece):
        whole = lax.all_gather(piece, "ctx", axis=0, tiled=True)
        return jnp.dot(features, whole, preferred_element_type=jnp.float32)

    query = (project(w_query) * 0.0625).astype(jnp.bfloat16)
    keys = project(key_matrix).astype(jnp.bfloat16)
    values = project(value_matrix).astype(jnp.bfloat16)
    blocks = WINDOW // rows_here
    joined = [jnp.concatenate([keys, values], axis=1)]
    for _ in range(blocks):
        joined = [shifted(joined[0], "ctx", 1)] + joined
    lead = (lax.axis_index("ctx") * rows_here).astype(jnp.int32).reshape(1)
    attended, shares = attend(query, d_attended, joined, lead, doc_lengths, 0, kv_heads)
    total = shares[0]
    for share in shares[1:-1]:
        moved = shifted(total, "ctx", -1).astype(jnp.float32)
        total = (moved + share.astype(jnp.float32)).astype(jnp.bfloat16)
    key_grad = shifted(total, "ctx", -1).astype(jnp.float32) + shares[-1]
    return (attended, key_grad.astype(jnp.bfloat16))


def solution(mesh):
    return jax.shard_map(
        local,
        mesh=mesh,
        in_specs=(
            P("ctx", "head"),
            P("ctx", "head"),
            P("ctx", "head"),
            P("ctx", "head"),
            P("ctx", "head"),
            P(),
        ),
        out_specs=(P("ctx", "head"), P("ctx", "head")),
        check_vma=False,
    )
```

```python
import functools

import jax
import jax.numpy as jnp
from jax import lax
from jax.experimental import pallas as pl
from jax.experimental.pallas import tpu as pltpu
from jax.sharding import Mesh
from jax.sharding import PartitionSpec as P

HEAD_SIZE = 256
WINDOW = 1024
TILE = 128


def shifted(block, axis, distance):
    devices = range(lax.axis_size("chip") * lax.axis_size("core"))
    route = [(i - distance, i) for i in devices if i - distance in devices]
    return lax.ppermute(block, axis, route)


def attend_kernel(count, group, *refs):
    lead_ref, lengths_ref, query_ref, grad_ref = refs[:4]
    key_refs = refs[4 : 4 + count]
    value_refs = refs[4 + count : 4 + 2 * count]
    out_ref = refs[4 + 2 * count]
    sum_refs = refs[5 + 2 * count : 5 + 3 * count]
    keys, values, sums = refs[5 + 3 * count :]
    rows = query_ref.shape[0]
    docs = lengths_ref.shape[0]
    for n in range(count):
        keys[n * rows : (n + 1) * rows] = key_refs[n][...]
        values[n * rows : (n + 1) * rows] = value_refs[n][...]
    sums[...] = jnp.zeros_like(sums)
    lead = lead_ref[0]
    span = WINDOW + TILE

    def one_tile(t, carry):
        first = pl.multiple_of(t * TILE, TILE)
        window = pl.ds(first, span)
        row_pos = lead + first + lax.broadcasted_iota(jnp.int32, (TILE, 1), 0)
        key_pos = lead + first - WINDOW + lax.broadcasted_iota(jnp.int32, (1, span), 1)
        begin = jnp.zeros_like(row_pos)
        start = jnp.int32(0)
        for d in range(docs):
            begin = jnp.where(row_pos >= start, start, begin)
            start = start + lengths_ref[d]
        least = jnp.maximum(begin, row_pos - (WINDOW - 1))
        allowed = (key_pos >= least) & (key_pos <= row_pos)
        key = keys[window, :]
        value = values[window, :]
        total = sums[window, :]
        for e in range(group):
            columns = slice(e * HEAD_SIZE, (e + 1) * HEAD_SIZE)
            query = query_ref[pl.ds(first, TILE), columns]
            grad = grad_ref[pl.ds(first, TILE), columns]
            scores = lax.dot_general(
                query, key, (((1,), (1,)), ((), ())), preferred_element_type=jnp.float32
            )
            dprob = lax.dot_general(
                grad, value, (((1,), (1,)), ((), ())), preferred_element_type=jnp.float32
            )
            scores = jnp.where(allowed, scores, -1e30)
            expo = jnp.exp(scores - jnp.max(scores, axis=1, keepdims=True))
            probs = expo * (1.0 / jnp.sum(expo, axis=1, keepdims=True))
            out = jnp.dot(probs.astype(jnp.bfloat16), value, preferred_element_type=jnp.float32)
            out_ref[pl.ds(first, TILE), columns] = out.astype(jnp.bfloat16)
            delta = jnp.sum(probs * dprob, axis=1, keepdims=True)
            dscore = (probs * (dprob - delta)).astype(jnp.bfloat16)
            total = total + lax.dot_general(
                dscore, query, (((0,), (0,)), ((), ())), preferred_element_type=jnp.float32
            )
        sums[window, :] = total
        return carry

    lax.fori_loop(0, rows // TILE, one_tile, 0)
    for n in range(count):
        sum_refs[n][...] = sums[n * rows : (n + 1) * rows].astype(sum_refs[n].dtype)


def attend(query, grad_rows, joined, lead, lengths, first_head, heads):
    rows = query.shape[0]
    count = len(joined)
    kv_heads = joined[0].shape[1] // (2 * HEAD_SIZE)
    group = query.shape[1] // (kv_heads * HEAD_SIZE)
    wide = pl.BlockSpec((rows, group * HEAD_SIZE), lambda g: (0, first_head + g))
    key_spec = pl.BlockSpec((rows, HEAD_SIZE), lambda g: (0, first_head + g))
    value_spec = pl.BlockSpec((rows, HEAD_SIZE), lambda g: (0, kv_heads + first_head + g))
    sum_spec = pl.BlockSpec((rows, HEAD_SIZE), lambda g: (0, g))
    scalars = pl.BlockSpec(memory_space=pltpu.SMEM)
    kinds = [jnp.bfloat16] * (count - 1) + [jnp.float32]
    outs = pl.pallas_call(
        functools.partial(attend_kernel, count, group),
        grid=(heads,),
        in_specs=[scalars, scalars, wide, wide] + [key_spec] * count + [value_spec] * count,
        out_specs=[pl.BlockSpec((rows, group * HEAD_SIZE), lambda g: (0, g))] + [sum_spec] * count,
        out_shape=[jax.ShapeDtypeStruct((rows, heads * group * HEAD_SIZE), jnp.bfloat16)]
        + [jax.ShapeDtypeStruct((rows, heads * HEAD_SIZE), kind) for kind in kinds],
        scratch_shapes=[
            pltpu.VMEM((count * rows, HEAD_SIZE), jnp.bfloat16),
            pltpu.VMEM((count * rows, HEAD_SIZE), jnp.bfloat16),
            pltpu.VMEM((count * rows, HEAD_SIZE), jnp.float32),
        ],
        compiler_params=pltpu.CompilerParams(vmem_limit_bytes=40 * 2**20),
        cost_estimate=pl.CostEstimate(
            flops=10 * heads * group * rows * (WINDOW + TILE) * HEAD_SIZE,
            bytes_accessed=heads * rows * HEAD_SIZE * 2 * (3 * group + 5 * count),
            transcendentals=heads * group * rows * (WINDOW + TILE),
        ),
    )(lead, lengths, query, grad_rows, *joined, *joined)
    return outs[0], outs[1:]


def from_partner(block):
    return lax.ppermute(block, "core", [(0, 1), (1, 0)])


def in_core_order(own, other):
    first = lax.axis_index("core") == 0
    return jnp.where(first, own, other), jnp.where(first, other, own)


def gather_features(tokens):
    count, width = lax.axis_size("head"), tokens.shape[1]
    me = lax.axis_index("head")
    features = jnp.zeros((tokens.shape[0], count * width), tokens.dtype)
    features = lax.dynamic_update_slice(features, tokens, (0, me * width))
    for step in range(1, count):
        moved = lax.ppermute(tokens, "head", [(i, (i + step) % count) for i in range(count)])
        source = lax.rem(me - step + count, count)
        features = lax.dynamic_update_slice(features, moved, (0, source * width))
    return features


def half_columns(weights):
    half = weights.shape[1] // 2
    left, right = weights[:, :half], weights[:, half:]
    first = lax.axis_index("core") == 0
    keep, send = jnp.where(first, left, right), jnp.where(first, right, left)
    return jnp.concatenate(in_core_order(keep, from_partner(send)), axis=0)


def local(tokens, w_query, key_matrix, value_matrix, d_attended, doc_lengths):
    rows_here = tokens.shape[0]
    kv_heads = key_matrix.shape[1] // HEAD_SIZE
    features = gather_features(tokens)
    kv_piece = jnp.concatenate([half_columns(key_matrix), half_columns(value_matrix)], axis=1)
    kv_whole = lax.all_gather(kv_piece, "chip", axis=0, tiled=True)
    kv_whole, query_piece = lax.optimization_barrier((kv_whole, half_columns(w_query)))
    query_whole = lax.all_gather(query_piece, "chip", axis=0, tiled=True)
    theirs = from_partner(features)

    def project(whole, factor):
        mine = jnp.dot(features, whole, preferred_element_type=jnp.float32) * factor
        others = jnp.dot(theirs, whole, preferred_element_type=jnp.float32) * factor
        return in_core_order(mine.astype(jnp.bfloat16), from_partner(others.astype(jnp.bfloat16)))

    left, right = project(kv_whole, 1.0)
    half = key_matrix.shape[1] // 2
    blocks = WINDOW // rows_here
    joined = [jnp.concatenate([left[:, :half], right[:, :half], left[:, half:], right[:, half:]], axis=1)]
    for _ in range(blocks):
        joined = [shifted(joined[0], ("chip", "core"), 1)] + joined
    query = jnp.concatenate(project(query_whole, 0.0625), axis=1)
    lead = (lax.axis_index(("chip", "core")) * rows_here).astype(jnp.int32).reshape(1)
    attended, shares = attend(query, d_attended, joined, lead, doc_lengths, 0, kv_heads)
    total = shares[0]
    for share in shares[1:-1]:
        moved = shifted(total, ("chip", "core"), -1).astype(jnp.float32)
        total = (moved + share.astype(jnp.float32)).astype(jnp.bfloat16)
    key_grad = shifted(total, ("chip", "core"), -1).astype(jnp.float32) + shares[-1]
    return (attended, key_grad.astype(jnp.bfloat16))


def solution(mesh):
    positions, heads = mesh.devices.shape
    cores = Mesh(mesh.devices.reshape(positions // 2, 2, heads), ("chip", "core", "head"))
    split = P(("chip", "core"), "head")
    return jax.shard_map(
        local,
        mesh=cores,
        in_specs=(split, split, split, split, split, P()),
        out_specs=(split, split),
        check_vma=False,
    )
```

```python
import functools

import jax
import jax.numpy as jnp
from jax import lax
from jax.experimental import pallas as pl
from jax.experimental.pallas import tpu as pltpu
from jax.sharding import Mesh
from jax.sharding import PartitionSpec as P

HEAD_SIZE = 256
WINDOW = 1024
TILE = 128


def shifted(block, axis, distance):
    devices = range(lax.axis_size("chip") * lax.axis_size("core"))
    route = [(i - distance, i) for i in devices if i - distance in devices]
    return lax.ppermute(block, axis, route)


def attend_kernel(count, group, *refs):
    lead_ref, lengths_ref, query_ref, grad_ref = refs[:4]
    key_refs = refs[4 : 4 + count]
    value_refs = refs[4 + count : 4 + 2 * count]
    out_ref = refs[4 + 2 * count]
    sum_refs = refs[5 + 2 * count : 5 + 3 * count]
    keys, values, sums = refs[5 + 3 * count :]
    rows = query_ref.shape[0]
    docs = lengths_ref.shape[0]
    for n in range(count):
        keys[n * rows : (n + 1) * rows] = key_refs[n][...]
        values[n * rows : (n + 1) * rows] = value_refs[n][...]
    sums[...] = jnp.zeros_like(sums)
    lead = lead_ref[0]
    span = WINDOW + TILE

    def one_tile(t, carry):
        first = pl.multiple_of(t * TILE, TILE)
        window = pl.ds(first, span)
        row_pos = lead + first + lax.broadcasted_iota(jnp.int32, (TILE, 1), 0)
        key_pos = lead + first - WINDOW + lax.broadcasted_iota(jnp.int32, (1, span), 1)
        begin = jnp.zeros_like(row_pos)
        start = jnp.int32(0)
        for d in range(docs):
            begin = jnp.where(row_pos >= start, start, begin)
            start = start + lengths_ref[d]
        least = jnp.maximum(begin, row_pos - (WINDOW - 1))
        allowed = (key_pos >= least) & (key_pos <= row_pos)
        key = keys[window, :]
        value = values[window, :]
        total = sums[window, :]
        for e in range(group):
            columns = slice(e * HEAD_SIZE, (e + 1) * HEAD_SIZE)
            query = query_ref[pl.ds(first, TILE), columns]
            grad = grad_ref[pl.ds(first, TILE), columns]
            scores = lax.dot_general(
                query, key, (((1,), (1,)), ((), ())), preferred_element_type=jnp.float32
            )
            dprob = lax.dot_general(
                grad, value, (((1,), (1,)), ((), ())), preferred_element_type=jnp.float32
            )
            scores = jnp.where(allowed, scores, -1e30)
            expo = jnp.exp(scores - jnp.max(scores, axis=1, keepdims=True))
            probs = expo * (1.0 / jnp.sum(expo, axis=1, keepdims=True))
            out = jnp.dot(probs.astype(jnp.bfloat16), value, preferred_element_type=jnp.float32)
            out_ref[pl.ds(first, TILE), columns] = out.astype(jnp.bfloat16)
            delta = jnp.sum(probs * dprob, axis=1, keepdims=True)
            dscore = (probs * (dprob - delta)).astype(jnp.bfloat16)
            total = total + lax.dot_general(
                dscore, query, (((0,), (0,)), ((), ())), preferred_element_type=jnp.float32
            )
        sums[window, :] = total
        return carry

    lax.fori_loop(0, rows // TILE, one_tile, 0)
    for n in range(count):
        sum_refs[n][...] = sums[n * rows : (n + 1) * rows].astype(sum_refs[n].dtype)


def attend(query, grad_rows, joined, lead, lengths, first_head, heads):
    rows = query.shape[0]
    count = len(joined)
    kv_heads = joined[0].shape[1] // (2 * HEAD_SIZE)
    group = query.shape[1] // (kv_heads * HEAD_SIZE)
    wide = pl.BlockSpec((rows, group * HEAD_SIZE), lambda g: (0, first_head + g))
    key_spec = pl.BlockSpec((rows, HEAD_SIZE), lambda g: (0, first_head + g))
    value_spec = pl.BlockSpec((rows, HEAD_SIZE), lambda g: (0, kv_heads + first_head + g))
    sum_spec = pl.BlockSpec((rows, HEAD_SIZE), lambda g: (0, g))
    scalars = pl.BlockSpec(memory_space=pltpu.SMEM)
    kinds = [jnp.bfloat16] * (count - 1) + [jnp.float32]
    outs = pl.pallas_call(
        functools.partial(attend_kernel, count, group),
        grid=(heads,),
        in_specs=[scalars, scalars, wide, wide] + [key_spec] * count + [value_spec] * count,
        out_specs=[pl.BlockSpec((rows, group * HEAD_SIZE), lambda g: (0, g))] + [sum_spec] * count,
        out_shape=[jax.ShapeDtypeStruct((rows, heads * group * HEAD_SIZE), jnp.bfloat16)]
        + [jax.ShapeDtypeStruct((rows, heads * HEAD_SIZE), kind) for kind in kinds],
        scratch_shapes=[
            pltpu.VMEM((count * rows, HEAD_SIZE), jnp.bfloat16),
            pltpu.VMEM((count * rows, HEAD_SIZE), jnp.bfloat16),
            pltpu.VMEM((count * rows, HEAD_SIZE), jnp.float32),
        ],
        compiler_params=pltpu.CompilerParams(vmem_limit_bytes=40 * 2**20),
        cost_estimate=pl.CostEstimate(
            flops=10 * heads * group * rows * (WINDOW + TILE) * HEAD_SIZE,
            bytes_accessed=heads * rows * HEAD_SIZE * 2 * (3 * group + 5 * count),
            transcendentals=heads * group * rows * (WINDOW + TILE),
        ),
    )(lead, lengths, query, grad_rows, *joined, *joined)
    return outs[0], outs[1:]


def from_partner(block):
    return lax.ppermute(block, "core", [(0, 1), (1, 0)])


def in_core_order(own, other):
    first = lax.axis_index("core") == 0
    return jnp.where(first, own, other), jnp.where(first, other, own)


def gather_features(tokens):
    count, width = lax.axis_size("head"), tokens.shape[1]
    me = lax.axis_index("head")
    features = jnp.zeros((tokens.shape[0], count * width), tokens.dtype)
    features = lax.dynamic_update_slice(features, tokens, (0, me * width))
    for step in range(1, count):
        moved = lax.ppermute(tokens, "head", [(i, (i + step) % count) for i in range(count)])
        source = lax.rem(me - step + count, count)
        features = lax.dynamic_update_slice(features, moved, (0, source * width))
    return features


def half_columns(weights):
    half = weights.shape[1] // 2
    left, right = weights[:, :half], weights[:, half:]
    first = lax.axis_index("core") == 0
    keep, send = jnp.where(first, left, right), jnp.where(first, right, left)
    return jnp.concatenate(in_core_order(keep, from_partner(send)), axis=0)


def local(tokens, w_query, key_matrix, value_matrix, d_attended, doc_lengths):
    rows_here = tokens.shape[0]
    kv_heads = key_matrix.shape[1] // HEAD_SIZE
    features = gather_features(tokens)
    kv_piece = jnp.concatenate([half_columns(key_matrix), half_columns(value_matrix)], axis=1)
    kv_whole = lax.all_gather(kv_piece, "chip", axis=0, tiled=True)
    query_piece = half_columns(w_query) + features[:1, :1] * 0 + features[:1, -1:] * 0
    query_whole = lax.all_gather(query_piece, "chip", axis=0, tiled=True)
    theirs = from_partner(features)

    def project(whole, factor):
        mine = jnp.dot(features, whole, preferred_element_type=jnp.float32) * factor
        others = jnp.dot(theirs, whole, preferred_element_type=jnp.float32) * factor
        return in_core_order(mine.astype(jnp.bfloat16), from_partner(others.astype(jnp.bfloat16)))

    left, right = project(kv_whole, 1.0)
    half = key_matrix.shape[1] // 2
    blocks = WINDOW // rows_here
    joined = [jnp.concatenate([left[:, :half], right[:, :half], left[:, half:], right[:, half:]], axis=1)]
    for _ in range(blocks):
        joined = [shifted(joined[0], ("chip", "core"), 1)] + joined
    query = jnp.concatenate(project(query_whole, 0.0625), axis=1)
    lead = (lax.axis_index(("chip", "core")) * rows_here).astype(jnp.int32).reshape(1)
    parts = 2 if kv_heads % 2 == 0 else 1
    heads = kv_heads // parts
    outs, grads = [], []
    for part in range(parts):
        out, shares = attend(query, d_attended, joined, lead, doc_lengths, part * heads, heads)
        total = shares[0]
        for share in shares[1:-1]:
            moved = shifted(total, ("chip", "core"), -1).astype(jnp.float32)
            total = (moved + share.astype(jnp.float32)).astype(jnp.bfloat16)
        key_grad = shifted(total, ("chip", "core"), -1).astype(jnp.float32) + shares[-1]
        outs.append(out)
        grads.append(key_grad.astype(jnp.bfloat16))
    return (jnp.concatenate(outs, axis=1), jnp.concatenate(grads, axis=1))


def solution(mesh):
    positions, heads = mesh.devices.shape
    cores = Mesh(mesh.devices.reshape(positions // 2, 2, heads), ("chip", "core", "head"))
    split = P(("chip", "core"), "head")
    return jax.shard_map(
        local,
        mesh=cores,
        in_specs=(split, split, split, split, split, P()),
        out_specs=(split, split),
        check_vma=False,
    )
```

```python
import functools

import jax
import jax.numpy as jnp
from jax import lax
from jax.experimental import pallas as pl
from jax.experimental.pallas import tpu as pltpu
from jax.sharding import Mesh
from jax.sharding import PartitionSpec as P

HEAD_SIZE = 256
WINDOW = 1024
TILE = 256


def shifted(block, axis, distance):
    devices = range(lax.axis_size("chip") * lax.axis_size("core"))
    route = [(i - distance, i) for i in devices if i - distance in devices]
    return lax.ppermute(block, axis, route)


def attend_kernel(count, group, *refs):
    lead_ref, lengths_ref, query_ref, grad_ref = refs[:4]
    key_refs = refs[4 : 4 + count]
    value_refs = refs[4 + count : 4 + 2 * count]
    out_ref = refs[4 + 2 * count]
    sum_refs = refs[5 + 2 * count : 5 + 3 * count]
    keys, values, sums = refs[5 + 3 * count :]
    rows = query_ref.shape[0]
    docs = lengths_ref.shape[0]
    for n in range(count):
        keys[n * rows : (n + 1) * rows] = key_refs[n][...]
        values[n * rows : (n + 1) * rows] = value_refs[n][...]
    sums[...] = jnp.zeros_like(sums)
    lead = lead_ref[0]
    span = WINDOW + TILE

    def one_tile(t, carry):
        first = pl.multiple_of(t * TILE, TILE)
        window = pl.ds(first, span)
        row_pos = lead + first + lax.broadcasted_iota(jnp.int32, (TILE, 1), 0)
        key_pos = lead + first - WINDOW + lax.broadcasted_iota(jnp.int32, (1, span), 1)
        begin = jnp.zeros_like(row_pos)
        start = jnp.int32(0)
        for d in range(docs):
            begin = jnp.where(row_pos >= start, start, begin)
            start = start + lengths_ref[d]
        least = jnp.maximum(begin, row_pos - (WINDOW - 1))
        allowed = (key_pos >= least) & (key_pos <= row_pos)
        key = keys[window, :]
        value = values[window, :]
        total = sums[window, :]
        for e in range(group):
            columns = slice(e * HEAD_SIZE, (e + 1) * HEAD_SIZE)
            query = query_ref[pl.ds(first, TILE), columns]
            grad = grad_ref[pl.ds(first, TILE), columns]
            scores = lax.dot_general(
                query, key, (((1,), (1,)), ((), ())), preferred_element_type=jnp.float32
            )
            dprob = lax.dot_general(
                grad, value, (((1,), (1,)), ((), ())), preferred_element_type=jnp.float32
            )
            scores = jnp.where(allowed, scores, -1e30)
            expo = jnp.exp(scores - jnp.max(scores, axis=1, keepdims=True))
            probs = expo * (1.0 / jnp.sum(expo, axis=1, keepdims=True))
            out = jnp.dot(probs.astype(jnp.bfloat16), value, preferred_element_type=jnp.float32)
            out_ref[pl.ds(first, TILE), columns] = out.astype(jnp.bfloat16)
            delta = jnp.sum(probs * dprob, axis=1, keepdims=True)
            dscore = (probs * (dprob - delta)).astype(jnp.bfloat16)
            total = total + lax.dot_general(
                dscore, query, (((0,), (0,)), ((), ())), preferred_element_type=jnp.float32
            )
        sums[window, :] = total
        return carry

    lax.fori_loop(0, rows // TILE, one_tile, 0)
    for n in range(count):
        sum_refs[n][...] = sums[n * rows : (n + 1) * rows].astype(sum_refs[n].dtype)


def attend(query, grad_rows, joined, lead, lengths, first_head, heads):
    rows = query.shape[0]
    count = len(joined)
    kv_heads = joined[0].shape[1] // (2 * HEAD_SIZE)
    group = grad_rows.shape[1] // (kv_heads * HEAD_SIZE)
    query_spec = pl.BlockSpec((rows, group * HEAD_SIZE), lambda g: (0, g))
    wide = pl.BlockSpec((rows, group * HEAD_SIZE), lambda g: (0, first_head + g))
    key_spec = pl.BlockSpec((rows, HEAD_SIZE), lambda g: (0, first_head + g))
    value_spec = pl.BlockSpec((rows, HEAD_SIZE), lambda g: (0, kv_heads + first_head + g))
    sum_spec = pl.BlockSpec((rows, HEAD_SIZE), lambda g: (0, g))
    scalars = pl.BlockSpec(memory_space=pltpu.SMEM)
    kinds = [jnp.bfloat16] * (count - 1) + [jnp.float32]
    outs = pl.pallas_call(
        functools.partial(attend_kernel, count, group),
        grid=(heads,),
        in_specs=[scalars, scalars, query_spec, wide] + [key_spec] * count + [value_spec] * count,
        out_specs=[pl.BlockSpec((rows, group * HEAD_SIZE), lambda g: (0, g))] + [sum_spec] * count,
        out_shape=[jax.ShapeDtypeStruct((rows, heads * group * HEAD_SIZE), jnp.bfloat16)]
        + [jax.ShapeDtypeStruct((rows, heads * HEAD_SIZE), kind) for kind in kinds],
        scratch_shapes=[
            pltpu.VMEM((count * rows, HEAD_SIZE), jnp.bfloat16),
            pltpu.VMEM((count * rows, HEAD_SIZE), jnp.bfloat16),
            pltpu.VMEM((count * rows, HEAD_SIZE), jnp.float32),
        ],
        compiler_params=pltpu.CompilerParams(vmem_limit_bytes=40 * 2**20),
        cost_estimate=pl.CostEstimate(
            flops=10 * heads * group * rows * (WINDOW + TILE) * HEAD_SIZE,
            bytes_accessed=heads * rows * HEAD_SIZE * 2 * (3 * group + 5 * count),
            transcendentals=heads * group * rows * (WINDOW + TILE),
        ),
    )(lead, lengths, query, grad_rows, *joined, *joined)
    return outs[0], outs[1:]


def from_partner(block):
    return lax.ppermute(block, "core", [(0, 1), (1, 0)])


def in_core_order(own, other):
    first = lax.axis_index("core") == 0
    return jnp.where(first, own, other), jnp.where(first, other, own)


def gather_features(tokens):
    count, width = lax.axis_size("head"), tokens.shape[1]
    me = lax.axis_index("head")
    features = jnp.zeros((tokens.shape[0], count * width), tokens.dtype)
    features = lax.dynamic_update_slice(features, tokens, (0, me * width))
    for step in range(1, count):
        moved = lax.ppermute(tokens, "head", [(i, (i + step) % count) for i in range(count)])
        source = lax.rem(me - step + count, count)
        features = lax.dynamic_update_slice(features, moved, (0, source * width))
    return features


def half_columns(weights):
    half = weights.shape[1] // 2
    left, right = weights[:, :half], weights[:, half:]
    first = lax.axis_index("core") == 0
    keep, send = jnp.where(first, left, right), jnp.where(first, right, left)
    return jnp.concatenate(in_core_order(keep, from_partner(send)), axis=0)


def local(tokens, w_query, key_matrix, value_matrix, d_attended, doc_lengths):
    rows_here = tokens.shape[0]
    kv_heads = key_matrix.shape[1] // HEAD_SIZE
    features = gather_features(tokens)
    kv_piece = jnp.concatenate([half_columns(key_matrix), half_columns(value_matrix)], axis=1)
    kv_whole = lax.all_gather(kv_piece, "chip", axis=0, tiled=True)
    query_piece = half_columns(w_query) + features[:1, :1] * 0 + features[:1, -1:] * 0
    query_whole = lax.all_gather(query_piece, "chip", axis=0, tiled=True)
    theirs = from_partner(features)

    def project(whole, factor):
        mine = jnp.dot(features, whole, preferred_element_type=jnp.float32) * factor
        others = jnp.dot(theirs, whole, preferred_element_type=jnp.float32) * factor
        return in_core_order(mine.astype(jnp.bfloat16), from_partner(others.astype(jnp.bfloat16)))

    left, right = project(kv_whole, 1.0)
    half = key_matrix.shape[1] // 2
    blocks = WINDOW // rows_here
    joined = [jnp.concatenate([left[:, :half], right[:, :half], left[:, half:], right[:, half:]], axis=1)]
    for _ in range(blocks):
        joined = [shifted(joined[0], ("chip", "core"), 1)] + joined
    queries = project(query_whole, 0.0625)
    lead = (lax.axis_index(("chip", "core")) * rows_here).astype(jnp.int32).reshape(1)
    parts = 2 if kv_heads % 2 == 0 else 1
    heads = kv_heads // parts
    if parts == 1:
        queries = [jnp.concatenate(queries, axis=1)]
    outs, grads = [], []
    for part in range(parts):
        out, shares = attend(queries[part], d_attended, joined, lead, doc_lengths, part * heads, heads)
        total = shares[0]
        for share in shares[1:-1]:
            moved = shifted(total, ("chip", "core"), -1).astype(jnp.float32)
            total = (moved + share.astype(jnp.float32)).astype(jnp.bfloat16)
        key_grad = shifted(total, ("chip", "core"), -1).astype(jnp.float32) + shares[-1]
        outs.append(out)
        grads.append(key_grad.astype(jnp.bfloat16))
    return (jnp.concatenate(outs, axis=1), jnp.concatenate(grads, axis=1))


def solution(mesh):
    positions, heads = mesh.devices.shape
    cores = Mesh(mesh.devices.reshape(positions // 2, 2, heads), ("chip", "core", "head"))
    split = P(("chip", "core"), "head")
    return jax.shard_map(
        local,
        mesh=cores,
        in_specs=(split, split, split, split, split, P()),
        out_specs=(split, split),
        check_vma=False,
    )
```
